32 devices in a mesh: coil: 8 (over z, x), frame: 4 (over y, core).
Axes of the slice: x: 2, y: 2, z: 4, core: 2. Of those that a mesh axis runs over, the one named last changes fastest.
Arguments:
- kspace: bfloat16 [32, 1024, 8, 256], P('coil', 'frame'), may hold values from -6 to 6
- sampled_lines: int32 [1024, 8], P('frame'), may hold values from 0 to 63, all different within a row
- sensitivity: float32 [32, 2, 8192], P('coil'), may hold values from -55 to 55
- dictionary: bfloat16 [16384, 2048], P('coil'), may hold values from -55 to 55
- atom_params: float32 [6, 16384], P(None, 'coil'), may hold values from -4 to 4
- concentration: float32 [8192], P('frame'), may hold values from 20 to 3000
Outputs:
- estimates: float32 [6, 8192], P(None, 'frame')
The draws below stay inside these ranges and needn't reach their ends.
Inputs may be any that keep to these rules, and one draw needn't show every extreme that they name: `sampled_lines`: each frame names 8 different lines.
All inputs are finite; a program needn't handle non-finite values.
Results may differ from the reference program's by a relative error of at most 0.0025.
The reference program's roundings to bfloat16 on the way (of `fingerprints`) count: a program that leaves them out, or rounds other values in their place, can miss the bound.
Values may be sent and summed in bfloat16 or wider, within the bound.
A program may use at most 192 MiB of HBM per device.

```python
import math
import jax
import jax.numpy as jnp
from jax import lax

COILS = 32
FRAMES = 1024
NPE = 64
NRO = 128
LINES = 8
ROWS = 64
ATOMS = 16384
VOXELS = 8192


def draw_sensitivity(key, part):
    shape = (COILS, 2, VOXELS)
    values = jnp.clip(jax.random.normal(key, shape, jnp.float32), -5.5, 5.5)
    levels = jax.random.uniform(jax.random.fold_in(key, 7), (VOXELS,), jnp.float32, 0.0, math.log(10.0))
    return values * jnp.exp(levels)[None, None, :]


def draw_dictionary(key, part):
    shape = (ATOMS, 2 * FRAMES)
    values = jnp.clip(jax.random.normal(key, shape, jnp.float32), -5.5, 5.5)
    levels = jax.random.uniform(jax.random.fold_in(key, 11), (ATOMS, 1), jnp.float32, 0.0, math.log(10.0))
    return (values * jnp.exp(levels)).astype(jnp.bfloat16)


def draw_concentration(key, part):
    levels = jax.random.uniform(key, (VOXELS,), jnp.float32, math.log(20.0), math.log(100.0))
    values = jnp.exp(levels)
    return values


def level_of(own_key, extent, pieces, smallest, largest):
    level, own = 1.0, jax.random.fold_in(own_key, 6)
    for dim, blocks in pieces:
        steps = jnp.exp(jax.random.uniform(jax.random.fold_in(own, dim), (blocks,), jnp.float32, smallest / len(pieces), largest / len(pieces)))
        level = level * jnp.repeat(steps, extent[dim] // blocks).reshape([-1 if axis == dim else 1 for axis in range(len(extent))])
    return level


def picks_of(own_key, rows, number_of, top, lift):
    ranking = jax.random.permutation(jax.random.fold_in(own_key, 1), number_of)
    boost = ranking
    for power in range(3):
        boost = boost * boost // number_of
    boost = boost * lift // number_of
    lots = jax.random.randint(jax.random.fold_in(own_key, 2), (rows, number_of), 0, 4096) + boost
    fixed_rows = jax.random.permutation(jax.random.fold_in(own_key, 3), rows)[jnp.arange(number_of) % rows]
    lots = jnp.where(jnp.arange(rows)[:, None] == fixed_rows[None, :], 1 << 14, lots)
    merit = lots * number_of + jnp.arange(number_of)
    return lax.top_k(merit.astype(jnp.int32), top)[1].astype(jnp.int32)


def gaussian(key, shape, width, bound, cuts=(), held_as=jnp.bfloat16):
    drawn = width * jax.random.normal(key, shape, jnp.float32)
    if cuts:
        drawn = drawn * level_of(key, shape, cuts, -0.22, 0.18)
    return jnp.clip(drawn, -bound, bound).astype(held_as)


def setup_inputs(seed: int = 0) -> dict:
    key_of = jax.random.split(jax.random.key(seed), 7)
    kspace = gaussian(key_of[0], (COILS, FRAMES, LINES, 2 * NRO), 1.0, 6.0, ((0, 8), (1, 4)))
    sampled_lines = picks_of(key_of[1], FRAMES, NPE, LINES, 0)
    sensitivity = draw_sensitivity(jax.random.fold_in(key_of[6], 71), 0)
    dictionary = draw_dictionary(jax.random.fold_in(key_of[6], 71), 0)
    atom_params = gaussian(key_of[4], (6, ATOMS), 1.0, 4.0, ((1, 8),), jnp.float32)
    concentration = draw_concentration(jax.random.fold_in(key_of[6], 71), 0)
    return dict(kspace=kspace, sampled_lines=sampled_lines, sensitivity=sensitivity, dictionary=dictionary, atom_params=atom_params, concentration=concentration)


def readout_table(length):
    position = jnp.arange(length, dtype=jnp.int32)
    angles = (position[:, None] * position[None, :] % length).astype(jnp.float32) * (2.0 * math.pi / length)
    cos_table = jnp.cos(angles)
    sine_table = jnp.sin(angles)
    upper_half = jnp.concatenate([cos_table, sine_table], axis=1)
    lower_half = jnp.concatenate([-sine_table, cos_table], axis=1)
    return jnp.concatenate([upper_half, lower_half], axis=0).astype(jnp.bfloat16)

def line_phases(line_index, row_count, length):
    row_index = jnp.arange(row_count, dtype=jnp.int32)
    angles = (line_index[:, :, None] * row_index[None, None, :] % length).astype(jnp.float32) * (2.0 * math.pi / length)
    return (jnp.cos(angles), jnp.sin(angles))

def coil_images(samples, cos_lines, sine_lines, table):
    spread = jnp.dot(samples, table, preferred_element_type=jnp.float32)
    half_width = spread.shape[-1] // 2
    real_part = spread[..., :half_width]
    imag_part = spread[..., half_width:]
    highest = lax.Precision.HIGHEST
    image_re = jnp.einsum('fly,cflx->cfyx', cos_lines, real_part, precision=highest) - jnp.einsum('fly,cflx->cfyx', sine_lines, imag_part, precision=highest)
    image_im = jnp.einsum('fly,cflx->cfyx', sine_lines, real_part, precision=highest) + jnp.einsum('fly,cflx->cfyx', cos_lines, imag_part, precision=highest)
    return (image_re, image_im)

def combine(image_re, image_im, sensitivity):
    coil_count, frame_count, row_count, column_count = image_re.shape
    flat_re = image_re.reshape(coil_count, frame_count, row_count * column_count)
    flat_im = image_im.reshape(coil_count, frame_count, row_count * column_count)
    sens_re = sensitivity[:, 0][:, None, :]
    sens_im = sensitivity[:, 1][:, None, :]
    part_re = lax.optimization_barrier(jnp.sum(sens_re * flat_re + sens_im * flat_im, axis=0))
    part_im = lax.optimization_barrier(jnp.sum(sens_re * flat_im - sens_im * flat_re, axis=0))
    return jnp.stack([part_re, part_im], axis=1)

def atom_scales(dictionary):
    widened = dictionary.astype(jnp.float32)
    return lax.rsqrt(lax.optimization_barrier(jnp.mean(widened * widened, axis=1)) + 1e-06)

def match_stats(dictionary, atom_scale, atom_params, segment, local_kappa):
    frame_count = segment.shape[0]
    voxel_count = segment.shape[-1]
    direct = segment.reshape(2 * frame_count, voxel_count)
    turned = jnp.stack([segment[:, 1], -segment[:, 0]], axis=1).reshape(2 * frame_count, voxel_count)
    stacked = jnp.concatenate([direct, turned], axis=1)
    inner = jnp.dot(dictionary, stacked, preferred_element_type=jnp.float32)
    magnitude = jnp.sqrt(inner[:, :voxel_count] * inner[:, :voxel_count] + inner[:, voxel_count:] * inner[:, voxel_count:])
    widened = direct.astype(jnp.float32)
    voxel_scale = lax.rsqrt(lax.optimization_barrier(jnp.mean(widened * widened, axis=0)) + 1e-06)
    logits = magnitude * atom_scale[:, None] * (voxel_scale * local_kappa / (2.0 * frame_count))[None, :]
    peak_score = lax.optimization_barrier(jnp.max(logits, axis=0))
    weights = jnp.exp(logits - peak_score[None, :])
    total_weight = lax.optimization_barrier(jnp.sum(weights, axis=0))
    moments = jnp.dot(atom_params, weights, precision=lax.Precision.HIGHEST, preferred_element_type=jnp.float32)
    return (peak_score, total_weight, moments)

def reference(kspace, sampled_lines, sensitivity, dictionary, atom_params, concentration):
    cos_lines, sine_lines = line_phases(sampled_lines, ROWS, NPE)
    table = readout_table(NRO)

    def accumulate(running, coil_data):
        samples, coil_sens = coil_data
        image_re, image_im = coil_images(samples[None], cos_lines, sine_lines, table)
        return (running + combine(image_re, image_im, coil_sens[None]), None)
    start_sum = jnp.zeros((FRAMES, 2, VOXELS), jnp.float32)
    combined, _ = lax.scan(accumulate, start_sum, (kspace, sensitivity))
    fingerprints = combined.astype(jnp.bfloat16)
    atom_scale = atom_scales(dictionary)
    block_size = 256 if VOXELS % 256 == 0 else 128
    block_count = VOXELS // block_size
    blocked = jnp.moveaxis(fingerprints.reshape(FRAMES, 2, block_count, block_size), 2, 0)
    kappa_blocks = concentration.reshape(block_count, block_size)

    def one_block(inputs):
        segment, local_kappa = inputs
        peak_score, total_weight, moments = match_stats(dictionary, atom_scale, atom_params, segment, local_kappa)
        return moments / total_weight[None, :]
    results = lax.map(one_block, (blocked, kappa_blocks))
    return jnp.transpose(results, (1, 0, 2)).reshape(6, VOXELS)
```

```python
import math

import jax
import jax.numpy as jnp
from jax import lax
from jax.sharding import PartitionSpec as P

NPE = 64
NRO = 128
ROWS = 64


def readout_table(length):
    position = jnp.arange(length, dtype=jnp.int32)
    angles = (position[:, None] * position[None, :] % length).astype(jnp.float32) * (
        2.0 * math.pi / length
    )
    cos_table = jnp.cos(angles)
    sine_table = jnp.sin(angles)
    upper_half = jnp.concatenate([cos_table, sine_table], axis=1)
    lower_half = jnp.concatenate([-sine_table, cos_table], axis=1)
    return jnp.concatenate([upper_half, lower_half], axis=0).astype(jnp.bfloat16)


def line_phases(line_index, row_count, length):
    row_index = jnp.arange(row_count, dtype=jnp.int32)
    angles = (line_index.T[:, :, None] * row_index[None, None, :] % length).astype(
        jnp.float32
    ) * (2.0 * math.pi / length)
    return (jnp.cos(angles), jnp.sin(angles))


def split(value):
    high = lax.reduce_precision(value, 8, 7)
    return high.astype(jnp.bfloat16), (value - high).astype(jnp.bfloat16)


def combined_images(samples, sens, cos_lines, sine_lines, table):
    coils, lines, frames, _ = samples.shape
    half = table.shape[1] // 2
    turned = samples.reshape(coils, lines * frames, samples.shape[3])
    spread = jnp.einsum(
        "cmk,krx->xrcm", turned, table.reshape(-1, 2, half), preferred_element_type=jnp.float32
    )
    g_high, g_low = split(spread.reshape(half, 2 * coils, lines * frames))
    left = jnp.concatenate([g_high, g_low, g_high], axis=1)
    sens_re = sens[:, 0].transpose(2, 0, 1)
    sens_im = sens[:, 1].transpose(2, 0, 1)
    from_re = jnp.concatenate([sens_re, -sens_im, sens_im, sens_re], axis=2)
    from_im = jnp.concatenate([sens_im, sens_re, -sens_re, sens_im], axis=2)
    s_high, s_low = split(jnp.concatenate([from_re, from_im], axis=1))
    right = jnp.concatenate([s_high, s_high, s_low], axis=1)
    sums = jnp.einsum("xkm,xkn->xmn", left, right, preferred_element_type=jnp.float32)
    rows = sens.shape[2]
    sums = sums.reshape(half, lines, frames, 4 * rows)
    cosine = jnp.concatenate([cos_lines, cos_lines], axis=2)
    sine = jnp.concatenate([sine_lines, sine_lines], axis=2)
    total = jnp.sum(
        cosine[None] * sums[..., : 2 * rows] + sine[None] * sums[..., 2 * rows :], axis=1
    ).astype(jnp.bfloat16)
    return total.reshape(half, frames, 2, rows).transpose(2, 1, 3, 0)


def column_orders(entries, frames, frame_groups, coil_groups):
    place = jnp.arange(entries, dtype=jnp.int32)
    run = place // (2 * frames)
    within = place % (2 * frames)
    part = within // frames
    frame = within % frames
    start = (run % frame_groups) * coil_groups + run // frame_groups
    base = start * (2 * frames) + 2 * frame
    source = place[:, None]
    direct = (source == (base + part)[None, :]).astype(jnp.bfloat16)
    sign = jnp.where(part == 0, -1.0, 1.0).astype(jnp.bfloat16)
    turned = (source == (base + 1 - part)[None, :]).astype(jnp.bfloat16) * sign[None, :]
    return direct, turned


def body(kspace, sampled_lines, sensitivity, dictionary, atom_params, concentration):
    frame_groups = lax.axis_size("frame")
    coil_groups = lax.axis_size("coil")
    frame_index = lax.axis_index("frame")
    coil_index = lax.axis_index("coil")
    voxel_total = sensitivity.shape[2]
    block_size = voxel_total // frame_groups
    local_frames = kspace.shape[1]
    few_frames = local_frames // coil_groups
    coils = kspace.shape[0] * coil_groups
    atoms, entries = dictionary.shape

    quarter = lax.dynamic_slice_in_dim(sensitivity, frame_index * block_size, block_size, 2)
    all_sens = lax.all_gather(quarter, ("coil", "frame"), axis=0)
    all_sens = (
        all_sens.reshape(coil_groups, frame_groups, kspace.shape[0], 2, block_size)
        .transpose(0, 2, 3, 1, 4)
        .reshape(coils, 2, ROWS, NRO)
    )
    lines_here = lax.dynamic_slice_in_dim(sampled_lines, coil_index * few_frames, few_frames, 0)
    cos_lines, sine_lines = line_phases(lines_here, ROWS, NPE)
    table = readout_table(NRO)

    pieces = PIECES if few_frames % (8 * PIECES) == 0 else 1
    step = few_frames // pieces
    grouped = kspace.reshape(kspace.shape[0], coil_groups, few_frames, *kspace.shape[2:])
    images = []
    for piece in range(pieces):
        part = slice(piece * step, (piece + 1) * step)
        sent = grouped[:, :, part].transpose(1, 0, 3, 2, 4)
        samples = lax.all_to_all(sent, "coil", split_axis=0, concat_axis=0, tiled=True)
        samples = samples.reshape(coils, *sent.shape[2:])
        images.append(
            combined_images(samples, all_sens, cos_lines[:, part], sine_lines[:, part], table)
        )
    image = jnp.concatenate(images, axis=1) if pieces > 1 else images[0]
    local = image.reshape(2 * few_frames, frame_groups, block_size).transpose(1, 0, 2)
    routed = lax.all_to_all(local, "frame", split_axis=0, concat_axis=0, tiled=True)
    routed = routed.reshape(frame_groups * 2 * few_frames, block_size)

    direct, turned = column_orders(entries, few_frames, frame_groups, coil_groups)
    straight = jnp.dot(dictionary, direct, preferred_element_type=jnp.float32)
    crossed = jnp.dot(dictionary, turned, preferred_element_type=jnp.float32)
    straight = straight.astype(jnp.bfloat16)
    crossed = crossed.astype(jnp.bfloat16)
    widened = dictionary.astype(jnp.float32)
    atom_scale = lax.rsqrt(jnp.mean(widened * widened, axis=1) + 1e-06)
    weighted = jnp.concatenate(
        [jnp.ones((1, atoms), jnp.float32), atom_params], axis=0
    )

    parts = PARTS if block_size % (128 * PARTS) == 0 else 1
    share = block_size // parts
    statistics = []
    for number in range(parts):
        span = slice(number * share, (number + 1) * share)
        fingerprints = lax.all_gather(
            routed[:, span], "coil", axis=0, tiled=True
        )
        inner_re = jnp.dot(straight, fingerprints, preferred_element_type=jnp.float32)
        inner_im = jnp.dot(crossed, fingerprints, preferred_element_type=jnp.float32)
        magnitude = jnp.sqrt(inner_re * inner_re + inner_im * inner_im)
        long = fingerprints.astype(jnp.float32)
        voxel_scale = lax.rsqrt(jnp.mean(long * long, axis=0) + 1e-06)
        logits = (
            magnitude
            * atom_scale[:, None]
            * (voxel_scale * concentration[span] / entries)[None, :]
        )
        peak = jnp.max(logits, axis=0)
        weights = jnp.exp(logits - peak[None, :])
        sums = jnp.dot(
            weighted, weights, precision=lax.Precision.HIGHEST,
            preferred_element_type=jnp.float32,
        )
        statistics.append(jnp.concatenate([peak[None], sums], axis=0))
    statistics = jnp.concatenate(statistics, axis=1) if parts > 1 else statistics[0]
    spread = jnp.broadcast_to(statistics[None], (coil_groups, *statistics.shape))
    everyone = lax.all_to_all(spread, "coil", split_axis=0, concat_axis=0, tiled=True)
    peaks = everyone[:, 0]
    factor = jnp.exp(peaks - jnp.max(peaks, axis=0)[None])
    sums = jnp.sum(everyone[:, 1:] * factor[:, None, :], axis=0)
    return sums[1:] / sums[:1]


PIECES = 2
PARTS = 1


def solution(mesh):
    in_specs = (
        P("coil", "frame", None, None),
        P("frame", None),
        P("coil", None, None),
        P("coil", None),
        P(None, "coil"),
        P("frame"),
    )
    out_specs = P(None, "frame")
    return jax.shard_map(body, mesh=mesh, in_specs=in_specs, out_specs=out_specs, check_vma=False)
```

```python
import math

import jax
import jax.numpy as jnp
from jax import lax
from jax.sharding import PartitionSpec as P

NPE = 64
NRO = 128
ROWS = 64


def readout_table(length):
    position = jnp.arange(length, dtype=jnp.int32)
    angles = (position[:, None] * position[None, :] % length).astype(jnp.float32) * (
        2.0 * math.pi / length
    )
    cos_table = jnp.cos(angles)
    sine_table = jnp.sin(angles)
    upper_half = jnp.concatenate([cos_table, sine_table], axis=1)
    lower_half = jnp.concatenate([-sine_table, cos_table], axis=1)
    return jnp.concatenate([upper_half, lower_half], axis=0).astype(jnp.bfloat16)


def line_phases(line_index, row_count, length):
    row_index = jnp.arange(row_count, dtype=jnp.int32)
    angles = (line_index.T[:, :, None] * row_index[None, None, :] % length).astype(
        jnp.float32
    ) * (2.0 * math.pi / length)
    return (jnp.cos(angles), jnp.sin(angles))


def split(value):
    high = lax.reduce_precision(value, 8, 7)
    return high.astype(jnp.bfloat16), (value - high).astype(jnp.bfloat16)


def combined_images(samples, sens, cos_lines, sine_lines, table):
    coils, lines, frames, _ = samples.shape
    half = table.shape[1] // 2
    turned = samples.reshape(coils, lines * frames, samples.shape[3])
    spread = jnp.einsum(
        "cmk,krx->xrcm", turned, table.reshape(-1, 2, half), preferred_element_type=jnp.float32
    )
    g_high, g_low = split(spread.reshape(half, 2 * coils, lines * frames))
    left = jnp.concatenate([g_high, g_low, g_high], axis=1)
    sens_re = sens[:, 0].transpose(2, 0, 1)
    sens_im = sens[:, 1].transpose(2, 0, 1)
    from_re = jnp.concatenate([sens_re, -sens_im, sens_im, sens_re], axis=2)
    from_im = jnp.concatenate([sens_im, sens_re, -sens_re, sens_im], axis=2)
    s_high, s_low = split(jnp.concatenate([from_re, from_im], axis=1))
    right = jnp.concatenate([s_high, s_high, s_low], axis=1)
    sums = jnp.einsum("xkm,xkn->xmn", left, right, preferred_element_type=jnp.float32)
    rows = sens.shape[2]
    sums = sums.reshape(half, lines, frames, 4 * rows)
    cosine = jnp.concatenate([cos_lines, cos_lines], axis=2)
    sine = jnp.concatenate([sine_lines, sine_lines], axis=2)
    total = jnp.sum(
        cosine[None] * sums[..., : 2 * rows] + sine[None] * sums[..., 2 * rows :], axis=1
    ).astype(jnp.bfloat16)
    return total.reshape(half, frames, 2, rows).transpose(2, 1, 3, 0)


def ring_gather(block, ring):
    count = len(ring)
    ahead = [(ring[i], ring[(i + 1) % count]) for i in range(count)]
    back = [(there, here) for here, there in ahead]
    from_left, from_right = [block], [block]
    for step in range(count // 2):
        from_left.append(lax.ppermute(from_left[-1], "coil", ahead))
        if step < count - 1 - count // 2:
            from_right.append(lax.ppermute(from_right[-1], "coil", back))
    return jnp.concatenate(from_left + from_right[1:], axis=0)


def arrival_order(ring, coil_index):
    count = len(ring)
    places = [0] * count
    for place, group in enumerate(ring):
        places[group] = place
    here = jnp.asarray(places, jnp.int32)[coil_index]
    offsets = [-step for step in range(count // 2 + 1)]
    offsets += [step for step in range(1, count - count // 2)]
    return jnp.asarray(ring, jnp.int32)[(here + jnp.asarray(offsets, jnp.int32)) % count]


def column_orders(entries, frames, frame_groups, sources):
    coil_groups = sources.shape[0]
    place = jnp.arange(entries, dtype=jnp.int32)
    run = place // (2 * frames)
    within = place % (2 * frames)
    part = within // frames
    frame = within % frames
    start = (run % frame_groups) * coil_groups + sources[run // frame_groups]
    base = start * (2 * frames) + 2 * frame
    source = place[:, None]
    direct = (source == (base + part)[None, :]).astype(jnp.bfloat16)
    sign = jnp.where(part == 0, -1.0, 1.0).astype(jnp.bfloat16)
    turned = (source == (base + 1 - part)[None, :]).astype(jnp.bfloat16) * sign[None, :]
    return direct, turned


def body(kspace, sampled_lines, sensitivity, dictionary, atom_params, concentration):
    frame_groups = lax.axis_size("frame")
    coil_groups = lax.axis_size("coil")
    frame_index = lax.axis_index("frame")
    coil_index = lax.axis_index("coil")
    voxel_total = sensitivity.shape[2]
    block_size = voxel_total // frame_groups
    local_frames = kspace.shape[1]
    few_frames = local_frames // coil_groups
    coils = kspace.shape[0] * coil_groups
    atoms, entries = dictionary.shape

    quarter = lax.dynamic_slice_in_dim(sensitivity, frame_index * block_size, block_size, 2)
    all_sens = lax.all_gather(quarter, ("coil", "frame"), axis=0)
    all_sens = (
        all_sens.reshape(coil_groups, frame_groups, kspace.shape[0], 2, block_size)
        .transpose(0, 2, 3, 1, 4)
        .reshape(coils, 2, ROWS, NRO)
    )
    lines_here = lax.dynamic_slice_in_dim(sampled_lines, coil_index * few_frames, few_frames, 0)
    cos_lines, sine_lines = line_phases(lines_here, ROWS, NPE)
    table = readout_table(NRO)

    pieces = PIECES if few_frames % (8 * PIECES) == 0 else 1
    step = few_frames // pieces
    grouped = kspace.reshape(kspace.shape[0], coil_groups, few_frames, *kspace.shape[2:])
    images = []
    for piece in range(pieces):
        part = slice(piece * step, (piece + 1) * step)
        sent = grouped[:, :, part].transpose(1, 0, 3, 2, 4)
        if piece == 1:
            sent, all_sens = lax.optimization_barrier((sent, all_sens))
        samples = lax.all_to_all(sent, "coil", split_axis=0, concat_axis=0, tiled=True)
        samples = samples.reshape(coils, *sent.shape[2:])
        images.append(
            combined_images(samples, all_sens, cos_lines[:, part], sine_lines[:, part], table)
        )
    image = jnp.concatenate(images, axis=1) if pieces > 1 else images[0]
    local = image.reshape(2 * few_frames, frame_groups, block_size).transpose(1, 0, 2)
    routed = lax.all_to_all(local, "frame", split_axis=0, concat_axis=0, tiled=True)
    routed = routed.reshape(frame_groups * 2 * few_frames, block_size)

    ring = list(range(0, coil_groups, 2)) + list(range(1, coil_groups, 2))[::-1]
    sources = arrival_order(ring, coil_index)
    direct, turned = column_orders(entries, few_frames, frame_groups, sources)
    straight = jnp.dot(dictionary, direct, preferred_element_type=jnp.float32)
    crossed = jnp.dot(dictionary, turned, preferred_element_type=jnp.float32)
    straight = straight.astype(jnp.bfloat16)
    crossed = crossed.astype(jnp.bfloat16)
    widened = dictionary.astype(jnp.float32)
    atom_scale = lax.rsqrt(jnp.mean(widened * widened, axis=1) + 1e-06)
    weighted = jnp.concatenate(
        [jnp.ones((1, atoms), jnp.float32), atom_params], axis=0
    )

    parts = PARTS if block_size % (128 * PARTS) == 0 else 1
    share = block_size // parts
    statistics = []
    for number in range(parts):
        span = slice(number * share, (number + 1) * share)
        fingerprints = ring_gather(routed[:, span], ring)
        inner_re = jnp.dot(straight, fingerprints, preferred_element_type=jnp.float32)
        inner_im = jnp.dot(crossed, fingerprints, preferred_element_type=jnp.float32)
        magnitude = jnp.sqrt(inner_re * inner_re + inner_im * inner_im)
        long = fingerprints.astype(jnp.float32)
        voxel_scale = lax.rsqrt(jnp.mean(long * long, axis=0) + 1e-06)
        logits = (
            magnitude
            * atom_scale[:, None]
            * (voxel_scale * concentration[span] / entries)[None, :]
        )
        peak = jnp.max(logits, axis=0)
        weights = jnp.exp(logits - peak[None, :])
        sums = jnp.dot(
            weighted, weights, precision=lax.Precision.HIGHEST,
            preferred_element_type=jnp.float32,
        )
        statistics.append(jnp.concatenate([peak[None], sums], axis=0))
    statistics = jnp.concatenate(statistics, axis=1) if parts > 1 else statistics[0]
    spread = jnp.broadcast_to(statistics[None], (coil_groups, *statistics.shape))
    everyone = lax.all_to_all(spread, "coil", split_axis=0, concat_axis=0, tiled=True)
    peaks = everyone[:, 0]
    factor = jnp.exp(peaks - jnp.max(peaks, axis=0)[None])
    sums = jnp.sum(everyone[:, 1:] * factor[:, None, :], axis=0)
    return sums[1:] / sums[:1]


PIECES = 2
PARTS = 2


def solution(mesh):
    in_specs = (
        P("coil", "frame", None, None),
        P("frame", None),
        P("coil", None, None),
        P("coil", None),
        P(None, "coil"),
        P("frame"),
    )
    out_specs = P(None, "frame")
    return jax.shard_map(body, mesh=mesh, in_specs=in_specs, out_specs=out_specs, check_vma=False)
```
